32 devices in a mesh: row: 8 (over z, x), pair: 4 (over y, core).
Axes of the slice: x: 2, y: 2, z: 4, core: 2. Of those that a mesh axis runs over, the one named last changes fastest.
Arguments:
- snapshots: float32 [4096, 2048], P('row', 'pair'), may hold values from -16 to 16
- pairing: int32 [2, 16], replicated, may hold values from 0 to 15, as said below
Outputs:
- left_vectors: float32 [4096, 2048], P('row', 'pair')
- spectrum: float32 [2048], P('pair')
The draws below stay inside these ranges and needn't reach their ends.
Inputs may be any that keep to these rules, and one draw needn't show every extreme that they name: Each row of pairing is a permutation of 0 to 15; slots 2k and 2k + 1 of a row form a pair; no two blocks are paired in more than one round.
All inputs are finite; a program needn't handle non-finite values.
Results may differ from the reference program's by a relative error of at most 0.0003.
Values sent between devices are 32-bit elements; how exact they have to be, the bound alone decides.
No kernel may reach another device: no remote copies, remote signals or barrier semaphores. Data moves between devices by JAX's collectives and lax.ppermute only.
A program may use at most 64 MiB of HBM per device.

```python
import jax
import jax.numpy as jnp
from jax import lax

COLS = 2048
BLOCK = 128
ROUNDS = 2
EIG_ITERS = 3
BLOCKS = 16
ROWS = 4096


def draw_snapshots(key, part):
    key = jax.random.fold_in(key, 5)
    noise_key, factor_key, load_key = jax.random.split(key, 3)
    trend = 0.5 + 1.5 * jnp.arange(ROWS, dtype=jnp.float32) / ROWS
    noise = jax.random.normal(noise_key, (ROWS, COLS), jnp.float32)
    loading = jax.random.uniform(load_key, (COLS,), jnp.float32, -1.2, 1.2)
    factors = jax.random.normal(factor_key, (ROWS, 8), jnp.float32)
    shared = jnp.tile(factors, (1, COLS // 8))
    return jnp.clip(noise + trend[:, None] * loading[None, :] * shared, -16.0, 16.0)


def draw_pairing(key, part):
    key = jax.random.fold_in(key, 9)
    start_key, label_key, order_key, flip_key = jax.random.split(key, 4)
    final_label = BLOCKS - 1
    opening = jax.random.randint(start_key, (), 0, final_label)
    circle = (opening + jnp.arange(ROUNDS, dtype=jnp.int32)) % final_label
    pair_index = jnp.arange(BLOCKS // 2, dtype=jnp.int32)
    home_side = jnp.where(pair_index[None, :] == 0, final_label, (circle[:, None] + pair_index[None, :]) % final_label)
    away_side = jnp.where(pair_index[None, :] == 0, circle[:, None], (circle[:, None] - pair_index[None, :]) % final_label)
    labels = jax.random.permutation(label_key, BLOCKS)
    home_side = labels[home_side]
    away_side = labels[away_side]
    swapped = jax.random.randint(flip_key, (ROUNDS, BLOCKS // 2), 0, 2)
    leading = jnp.where(swapped == 1, away_side, home_side)
    trailing = jnp.where(swapped == 1, home_side, away_side)
    arranged = jnp.stack([leading, trailing], axis=-1)
    slot_order = jax.vmap(lambda subkey: jax.random.permutation(subkey, BLOCKS // 2))(jax.random.split(order_key, ROUNDS))
    arranged = jnp.take_along_axis(arranged, slot_order[:, :, None], axis=1)
    return arranged.reshape(ROUNDS, BLOCKS).astype(jnp.int32)


def setup_inputs(seed: int = 0) -> dict:
    seeds = jax.random.split(jax.random.key(seed), 3)
    snapshots = draw_snapshots(jax.random.fold_in(seeds[2], 71), 0)
    pairing = draw_pairing(jax.random.fold_in(seeds[2], 71), 0)
    return dict(snapshots=snapshots, pairing=pairing)


precise = lax.Precision.HIGHEST
epsilon = 1e-06

def orthogonal_factor(gram_pair):
    order_size = gram_pair.shape[-1]
    rotation = jnp.broadcast_to(jnp.eye(order_size, dtype=jnp.float32), gram_pair.shape)
    for iteration in range(EIG_ITERS):
        image = jnp.matmul(gram_pair, rotation, precision=precise)
        inner = jnp.matmul(jnp.swapaxes(image, -1, -2), image, precision=precise)
        factor_lower = jnp.linalg.cholesky(inner)
        solved = jax.scipy.linalg.solve_triangular(factor_lower, jnp.swapaxes(image, -1, -2), lower=True)
        rotation = jnp.swapaxes(solved, -1, -2)
    return rotation

def reference(snapshots, pairing):
    total_rows = snapshots.shape[0]
    blocks = snapshots.reshape(total_rows, BLOCKS, BLOCK).transpose(1, 0, 2)
    for sweep_index in range(ROUNDS):
        order_pairs = pairing[sweep_index].reshape(BLOCKS // 2, 2)
        for pair_index in range(BLOCKS // 2):
            first_block = order_pairs[pair_index, 0]
            second_block = order_pairs[pair_index, 1]
            joined = jnp.concatenate([blocks[first_block], blocks[second_block]], axis=1)
            gram_pair = jnp.dot(joined.T.astype(jnp.float32), joined.astype(jnp.float32), precision=precise, preferred_element_type=jnp.float32)
            rotation = orthogonal_factor(gram_pair)
            rotated = jnp.dot(joined.astype(jnp.float32), rotation.astype(jnp.float32), precision=precise, preferred_element_type=jnp.float32)
            blocks = blocks.at[first_block].set(rotated[:, :BLOCK])
            blocks = blocks.at[second_block].set(rotated[:, BLOCK:])
    squares = lax.optimization_barrier(jnp.sum(blocks * blocks, axis=1))
    spectrum = jnp.sqrt(squares / total_rows + epsilon)
    left_vectors = blocks / spectrum[:, None, :]
    left_vectors = left_vectors.transpose(1, 0, 2).reshape(total_rows, COLS)
    return (left_vectors, spectrum.reshape(COLS))
```

```python
import functools

import jax
import jax.numpy as jnp
from jax import lax
from jax.experimental import pallas as pl
from jax.experimental.pallas import tpu as pltpu
from jax.sharding import PartitionSpec as P

BLOCK = 128
ROUNDS = 2
EIG_ITERS = 3
SUB = 8

precise = lax.Precision.HIGHEST
epsilon = 1e-06
VMEM_LIMIT = 48 * 1024 * 1024


def mm(a, b):
    return lax.dot_general(
        a, b, (((1,), (0,)), ((), ())), precision=precise, preferred_element_type=jnp.float32
    )


def mm_nt(a, b):
    return lax.dot_general(
        a, b, (((1,), (1,)), ((), ())), precision=precise, preferred_element_type=jnp.float32
    )


def mm_tn(a, b):
    return lax.dot_general(
        a, b, (((0,), (0,)), ((), ())), precision=precise, preferred_element_type=jnp.float32
    )


def sub_row(v, t):
    return jnp.broadcast_to(v[t : t + 1, :], v.shape)


def lane_col(v, l):
    return jnp.broadcast_to(v[:, l : l + 1], v.shape)


def inverse_factor(matrix):
    groups = BLOCK // SUB
    shape = (SUB, BLOCK)
    sub = lax.broadcasted_iota(jnp.int32, shape, 0)
    lane = lax.broadcasted_iota(jnp.int32, shape, 1)
    strips = [matrix[SUB * g : SUB * (g + 1), :] for g in range(groups)]
    out = []
    for k in range(groups):
        first = SUB * k
        inside = (lane >= first) & (lane < first + SUB)
        strip = strips[k]
        cols = [lane_col(strip, first + s) for s in range(SUB)]
        below = {g: [lane_col(strips[g], first + s) for s in range(SUB)] for g in range(k + 1, groups)}
        strip = jnp.where(inside, jnp.where(lane == sub + first, 1.0, 0.0), strip)
        pivots = jnp.zeros(shape, jnp.float32)
        recips, scalars, rows = [], [], []
        for t in range(SUB):
            pivot = sub_row(cols[t], t)
            recip = 1.0 / pivot
            pivots = jnp.where(sub == t, pivot, pivots)
            masked = jnp.where(sub > t, cols[t], 0.0)
            row = sub_row(strip, t)
            scalar = {}
            for s in range(t + 1, SUB):
                scalar[s] = sub_row(cols[s], t)
                cols[s] = cols[s] - (masked * scalar[s]) * recip
            if t < SUB - 1:
                strip = strip - (masked * recip) * row
            recips.append(recip)
            scalars.append(scalar)
            rows.append(row)
        for g in range(k + 1, groups):
            col = below[g]
            rest = jnp.where(inside, 0.0, strips[g])
            for t in range(SUB):
                factor = col[t] * recips[t]
                for s in range(t + 1, SUB):
                    col[s] = col[s] - factor * scalars[t][s]
                rest = rest - factor * rows[t]
            strips[g] = rest
        out.append(jnp.where(lane < first + SUB, strip, 0.0) * lax.rsqrt(pivots))
    return jnp.concatenate(out, axis=0)


def step(gram, turned):
    image = gram if turned is None else mm(turned, gram)
    inner = mm_nt(image, image)
    upper_inv = inverse_factor(inner[:BLOCK, :BLOCK])
    corner = mm_nt(inner[BLOCK:, :BLOCK], upper_inv)
    lower_inv = inverse_factor(inner[BLOCK:, BLOCK:] - mm_nt(corner, corner))
    first = mm(upper_inv, image[:BLOCK])
    second = mm(lower_inv, image[BLOCK:] - mm(corner, first))
    return first, second


def store_step(out_ref, gram, turned):
    first, second = step(gram, turned)
    out_ref[:BLOCK, :] = first
    out_ref[BLOCK:, :] = second


def opening_kernel(parts_ref, gram_ref, out_ref):
    a11, a12, a22 = parts_ref[:BLOCK], parts_ref[BLOCK : 2 * BLOCK], parts_ref[2 * BLOCK :]
    gram_ref[:BLOCK, :BLOCK] = a11
    gram_ref[:BLOCK, BLOCK:] = a12
    gram_ref[BLOCK:, :BLOCK] = a12.T
    gram_ref[BLOCK:, BLOCK:] = a22
    store_step(out_ref, gram_ref[...], None)


def step_kernel(gram_ref, turned_ref, out_ref):
    store_step(out_ref, gram_ref[...], turned_ref[...])


def last_kernel(total_rows, gram_ref, turned_ref, out_ref, spec_ref):
    gram = gram_ref[...]
    first, second = step(gram, turned_ref[...])
    turned = jnp.concatenate([first, second], axis=0)
    squares = mm_nt(mm(turned, gram), turned)
    order = 2 * BLOCK
    diagonal = lax.broadcasted_iota(jnp.int32, (order, order), 0) == lax.broadcasted_iota(
        jnp.int32, (order, order), 1
    )
    squares = jnp.where(diagonal, squares, 0.0)
    along_rows = jnp.sqrt(jnp.sum(squares, axis=1, keepdims=True) / total_rows + epsilon)
    along_lanes = jnp.sqrt(jnp.sum(squares, axis=0, keepdims=True) / total_rows + epsilon)
    out_ref[...] = turned / along_rows
    spec_ref[...] = jnp.broadcast_to(along_lanes, spec_ref.shape)


def fetch_all(copies):
    for copy in copies:
        copy.start()
    for copy in copies:
        copy.wait()


def block_copies(parts, held, sems, place, slots):
    copies = []
    for d, part in enumerate(parts):
        for j in range(slots):
            copies.append(
                pltpu.make_async_copy(
                    part.at[:, j * BLOCK : (j + 1) * BLOCK],
                    held.at[(place ^ d) * slots + j],
                    sems.at[d * slots + j],
                )
            )
    return copies


def own_gram_kernel(slots, table, *refs):
    *parts, out_ref, held, sems = refs
    place = table[4, 0]
    fetch_all(block_copies(parts, held, sems, place, slots))
    for s in range(slots // 2):
        pair = place * (slots // 2) + s
        lead, trail = held[table[0, 2 * pair]], held[table[0, 2 * pair + 1]]
        out_ref[s, :BLOCK] = mm_tn(lead, lead)
        out_ref[s, BLOCK : 2 * BLOCK] = mm_tn(lead, trail)
        out_ref[s, 2 * BLOCK :] = mm_tn(trail, trail)


def cross_gram_kernel(slots, table, *refs):
    *parts, out_ref, held, sems = refs
    place = table[4, 0]
    fetch_all(block_copies(parts, held, sems, place, slots))
    for s in range(slots // 2):
        pair = place * (slots // 2) + s
        sides = []
        for side in range(2):
            source = table[2, table[1, 2 * pair + side]] // 2
            sides.append([held[table[0, 2 * source]], held[table[0, 2 * source + 1]]])
        for i in range(2):
            for j in range(2):
                out_ref[s, i * BLOCK : (i + 1) * BLOCK, j * BLOCK : (j + 1) * BLOCK] = mm_tn(
                    sides[0][i], sides[1][j]
                )


def joint_gram_kernel(count, table, *refs):
    turned_parts, gram_parts = refs[:count], refs[count : 2 * count]
    cross_ref, out_ref, turned, grams, sems = refs[2 * count :]
    owner = table[4, 1]
    copies = []
    for d in range(count):
        copies.append(pltpu.make_async_copy(turned_parts[d], turned.at[owner ^ d], sems.at[d]))
        copies.append(pltpu.make_async_copy(gram_parts[d], grams.at[owner ^ d], sems.at[count + d]))
    fetch_all(copies)
    halves = []
    for side in range(2):
        slot = table[2, table[1, 2 * owner + side]]
        source = slot // 2
        start = pl.multiple_of((slot % 2) * BLOCK, BLOCK)
        half = turned[source, pl.ds(start, BLOCK), :]
        halves.append(half)
        a11 = grams[source, :BLOCK]
        a12 = grams[source, BLOCK : 2 * BLOCK]
        a22 = grams[source, 2 * BLOCK :]
        whole = jnp.concatenate(
            [jnp.concatenate([a11, a12], axis=1), jnp.concatenate([a12.T, a22], axis=1)], axis=0
        )
        out_ref[2 * side * BLOCK : (2 * side + 1) * BLOCK] = mm_nt(mm(half, whole), half)
    out_ref[BLOCK : 2 * BLOCK] = mm_nt(mm(halves[0], cross_ref[...]), halves[1])


def first_turn_kernel(slots, count, table, *refs):
    parts, turned_parts = refs[: count // 2], refs[count // 2 : count // 2 + count]
    out_ref, held, turned, sems = refs[count // 2 + count :]
    place, owner = table[4, 0], table[4, 1]
    copies = block_copies(parts, held, sems, place, slots)
    for d in range(count):
        copies.append(
            pltpu.make_async_copy(turned_parts[d], turned.at[owner ^ d], sems.at[len(parts) * slots + d])
        )
    fetch_all(copies)
    for j in range(slots):
        pair = table[3, place * slots + j] // 2
        for side in range(2):
            slot = table[2, table[1, 2 * pair + side]]
            source = slot // 2
            start = pl.multiple_of((slot % 2) * BLOCK, BLOCK)
            half = turned[source, pl.ds(start, BLOCK), :]
            lead, trail = held[table[0, 2 * source]], held[table[0, 2 * source + 1]]
            out_ref[j, :, side * BLOCK : (side + 1) * BLOCK] = mm_nt(lead, half[:, :BLOCK]) + mm_nt(
                trail, half[:, BLOCK:]
            )


def last_turn_kernel(slots, count, table, *refs):
    columns_ref = refs[0]
    turned_parts, spec_parts = refs[1 : 1 + count], refs[1 + count : 1 + 2 * count]
    left_ref, spec_ref, turned, spec, sems = refs[1 + 2 * count :]
    place, owner = table[4, 0], table[4, 1]
    copies = []
    for d in range(count):
        copies.append(pltpu.make_async_copy(turned_parts[d], turned.at[owner ^ d], sems.at[d]))
        copies.append(pltpu.make_async_copy(spec_parts[d], spec.at[owner ^ d], sems.at[count + d]))
    fetch_all(copies)
    for j in range(slots):
        slot = table[3, place * slots + j]
        pair = slot // 2
        start = pl.multiple_of((slot % 2) * BLOCK, BLOCK)
        left_ref[:, j * BLOCK : (j + 1) * BLOCK] = mm_nt(
            columns_ref[j], turned[pair, pl.ds(start, BLOCK), :]
        )
        spec_ref[:, j * BLOCK : (j + 1) * BLOCK] = spec[pair, :, pl.ds(start, BLOCK)]


def exchange(x, axis, bit):
    size = lax.axis_size(axis)
    return lax.ppermute(x, axis, [(i, i ^ bit) for i in range(size)])


def gather_pairwise(x):
    parts = [x]
    bit = lax.axis_size("pair") // 2
    far = []
    while bit:
        fresh = [exchange(part, "pair", bit) for part in parts]
        far.append((bit, fresh))
        parts = parts + fresh
        bit //= 2
    order = [0]
    for bit, fresh in far:
        order = order + [o ^ bit for o in order]
    return [parts[order.index(d)] for d in range(len(parts))]


def gather_owners(x):
    parts = [x, exchange(x, "row", 1)]
    result = {0: parts[0], 1: parts[1]}
    bit = lax.axis_size("pair") // 2
    while bit:
        for d, part in list(result.items()):
            result[d ^ (2 * bit)] = exchange(part, "pair", bit)
        bit //= 2
    return [result[d] for d in range(len(result))]


def sum_rows(both, low):
    own = lax.dynamic_index_in_dim(both, low, keepdims=False)
    other = lax.dynamic_index_in_dim(both, 1 - low, keepdims=False)
    total = own + exchange(other, "row", 1)
    bit = 2
    while bit < lax.axis_size("row"):
        total = total + exchange(total, "row", bit)
        bit *= 2
    return total


vmem = pl.BlockSpec(memory_space=pltpu.VMEM)
smem = pl.BlockSpec(memory_space=pltpu.SMEM)
hbm = pl.BlockSpec(memory_space=pl.ANY)


def call(kernel, in_specs, out_shapes, scratch=(), name=None, flops=0):
    return pl.pallas_call(
        kernel,
        out_shape=[jax.ShapeDtypeStruct(s, jnp.float32) for s in out_shapes],
        in_specs=in_specs,
        out_specs=[vmem] * len(out_shapes),
        scratch_shapes=list(scratch),
        compiler_params=pltpu.CompilerParams(vmem_limit_bytes=VMEM_LIMIT),
        cost_estimate=pl.CostEstimate(flops=flops, bytes_accessed=1 << 20, transcendentals=0),
        name=name,
    )


def shards(snapshots, pairing):
    rows_dev, cols_dev = snapshots.shape
    slots = cols_dev // BLOCK
    places = lax.axis_size("pair")
    blocks = places * slots
    count = 2 * places
    total_rows = rows_dev * lax.axis_size("row")
    order = 2 * BLOCK
    place = lax.axis_index("pair")
    low = lax.axis_index("row") % 2
    owner = place * 2 + low
    ids = jnp.arange(blocks, dtype=jnp.int32)
    where = jnp.sum(
        jnp.where(pairing[:, :, None] == ids[None, None, :], ids[None, :, None], 0), axis=1
    ).astype(jnp.int32)
    own_ids = jnp.where(ids == 0, place, jnp.where(ids == 1, owner, 0)).astype(jnp.int32)
    table = jnp.concatenate([pairing, where, own_ids[None]], axis=0)

    f32 = jnp.float32
    held = pltpu.VMEM((blocks, rows_dev, BLOCK), f32)
    parts = gather_pairwise(snapshots)
    dma = pltpu.SemaphoreType.DMA
    half = slots // 2
    (own_grams,) = call(
        functools.partial(own_gram_kernel, slots),
        [smem] + [hbm] * places,
        [(half, 3 * BLOCK, BLOCK)],
        [held, dma((blocks,))],
        "own_gram",
    )(table, *parts)
    (cross_grams,) = call(
        functools.partial(cross_gram_kernel, slots),
        [smem] + [hbm] * places,
        [(half, order, order)],
        [held, dma((blocks,))],
        "cross_gram",
    )(table, *parts)
    own_gram = sum_rows(own_grams, low)
    cross_gram = sum_rows(cross_grams, low)
    gram_parts = gather_owners(own_gram)

    chain = 1 << 33
    square = (order, order)

    def rotate(gram_pieces, last):
        gram, turned = call(opening_kernel, [vmem], [square, square], (), "opening_step", chain)(gram_pieces)
        for iteration in range(1, EIG_ITERS):
            if last and iteration == EIG_ITERS - 1:
                return call(
                    functools.partial(last_kernel, total_rows),
                    [vmem, vmem],
                    [square, (SUB, order)],
                    (),
                    "last_step",
                    chain,
                )(gram, turned)
            (turned,) = call(step_kernel, [vmem, vmem], [square], (), "inner_step", chain)(gram, turned)
        return turned

    turned = rotate(own_gram, False)
    turned_parts = gather_owners(turned)
    (joint_gram,) = call(
        functools.partial(joint_gram_kernel, count),
        [smem] + [hbm] * (2 * count) + [vmem],
        [(3 * BLOCK, BLOCK)],
        [
            pltpu.VMEM((count,) + square, f32),
            pltpu.VMEM((count, 3 * BLOCK, BLOCK), f32),
            dma((2 * count,)),
        ],
        "joint_gram",
    )(table, *turned_parts, *gram_parts, cross_gram)
    second, spec = rotate(joint_gram, True)
    (columns,) = call(
        functools.partial(first_turn_kernel, slots, count),
        [smem] + [hbm] * (places + count),
        [(slots, rows_dev, order)],
        [held, pltpu.VMEM((count,) + square, f32), dma((blocks + count,))],
        "first_turn",
    )(table, *parts, *turned_parts)
    second_parts = gather_owners(second)
    spec_parts = gather_owners(spec)
    left, spectrum = call(
        functools.partial(last_turn_kernel, slots, count),
        [smem, vmem] + [hbm] * (2 * count),
        [(rows_dev, cols_dev), (SUB, cols_dev)],
        [
            pltpu.VMEM((count,) + square, f32),
            pltpu.VMEM((count, SUB, order), f32),
            dma((2 * count,)),
        ],
        "last_turn",
    )(table, columns, *second_parts, *spec_parts)
    return left, spectrum[0]


def solution(mesh):
    return jax.shard_map(
        shards,
        mesh=mesh,
        in_specs=(P("row", "pair"), P()),
        out_specs=(P("row", "pair"), P("pair")),
        check_vma=False,
    )
```

```python
import functools

import jax
import jax.numpy as jnp
from jax import lax
from jax.experimental import pallas as pl
from jax.experimental.pallas import tpu as pltpu
from jax.sharding import PartitionSpec as P

BLOCK = 128
ROUNDS = 2
EIG_ITERS = 3
SUB = 8

precise = lax.Precision.HIGHEST
epsilon = 1e-06
VMEM_LIMIT = 24 * 1024 * 1024
PACK = BLOCK // 4
HALF_ROWS = BLOCK + PACK
STEP_ROWS = 2 * HALF_ROWS + SUB
PACK_PLACES = ((BLOCK, 0), (BLOCK, BLOCK), (HALF_ROWS + BLOCK, 0), (HALF_ROWS + BLOCK, BLOCK))
ALONE = (64, 2)
PAIRED = (32, 1)


def mm(a, b):
    return lax.dot_general(
        a, b, (((1,), (0,)), ((), ())), precision=precise, preferred_element_type=jnp.float32
    )


def mm_nt(a, b):
    return lax.dot_general(
        a, b, (((1,), (1,)), ((), ())), precision=precise, preferred_element_type=jnp.float32
    )


def mm_tn(a, b):
    return lax.dot_general(
        a, b, (((0,), (0,)), ((), ())), precision=precise, preferred_element_type=jnp.float32
    )


def halves_of(x):
    high = x.astype(jnp.bfloat16)
    return high, (x - high.astype(jnp.float32)).astype(jnp.bfloat16)


def mm_nt_three(a, b):
    def one(x, y):
        return lax.dot_general(x, y, (((1,), (1,)), ((), ())), preferred_element_type=jnp.float32)

    (a_high, a_low), (b_high, b_low) = halves_of(a), halves_of(b)
    return one(a_high, b_high) + (one(a_high, b_low) + one(a_low, b_high))


def sub_row(v, t):
    return jnp.broadcast_to(v[t : t + 1, :], v.shape)


def lane_col(v, l):
    return jnp.broadcast_to(v[:, l : l + 1], v.shape)


def factor_steps(matrix, panel, ahead):
    groups, strips_panel = BLOCK // SUB, panel // SUB
    shape = (SUB, BLOCK)
    sub = lax.broadcasted_iota(jnp.int32, shape, 0)
    lane = lax.broadcasted_iota(jnp.int32, shape, 1)
    strips = [matrix[SUB * g : SUB * (g + 1), :] for g in range(groups)]
    out = []
    for opening in range(0, groups, strips_panel):
        end = opening + strips_panel
        next_cols = next_below = None
        finished = []
        for k in range(opening, end):
            first = SUB * k
            inside = (lane >= first) & (lane < first + SUB)
            strip = strips[k]
            cols = next_cols
            if cols is None:
                cols = [lane_col(strip, first + s) for s in range(SUB)]
            below = {}
            for g in range(k + 1, end):
                if g == k + 1 and next_below is not None:
                    below[g] = next_below
                else:
                    below[g] = [lane_col(strips[g], first + s) for s in range(SUB)]
            next_cols = next_below = None
            if ahead >= 1 and k + 1 < end:
                next_cols = [lane_col(strips[k + 1], first + SUB + s) for s in range(SUB)]
            if ahead >= 2 and k + 2 < end:
                next_below = [lane_col(strips[k + 2], first + SUB + s) for s in range(SUB)]
            strip = jnp.where(inside, jnp.where(lane == sub + first, 1.0, 0.0), strip)
            recips = jnp.zeros(shape, jnp.float32)
            recip, scalars, rows = [], [], []
            yield
            for t in range(SUB):
                r = 1.0 / sub_row(cols[t], t)
                recips = jnp.where(sub == t, r, recips)
                masked = jnp.where(sub > t, cols[t], 0.0)
                factor = masked * r
                row = sub_row(strip, t)
                scalar = {}
                for s in range(t + 1, SUB):
                    scalar[s] = sub_row(cols[s], t)
                    cols[s] = cols[s] - ((masked * scalar[s]) * r if s == t + 1 else factor * scalar[s])
                if t < SUB - 1:
                    strip = strip - factor * row
                recip.append(r)
                scalars.append(scalar)
                rows.append(row)
                if next_cols is not None:
                    col = below[k + 1]
                    factor = col[t] * r
                    for s in range(t + 1, SUB):
                        col[s] = col[s] - factor * scalar[s]
                    across = [sub_row(col[t], s) for s in range(SUB)]
                    for s in range(SUB):
                        next_cols[s] = next_cols[s] - factor * across[s]
                    if next_below is not None:
                        col = below[k + 2]
                        factor = col[t] * r
                        for s in range(t + 1, SUB):
                            col[s] = col[s] - factor * scalar[s]
                        for s in range(SUB):
                            next_below[s] = next_below[s] - factor * across[s]
                yield
            for g in range(k + 1, end):
                col = below[g]
                done = (g == k + 1 and next_cols is not None) or (g == k + 2 and next_below is not None)
                rest = jnp.where(inside, 0.0, strips[g])
                for t in range(SUB):
                    factor = col[t] * recip[t]
                    if not done:
                        for s in range(t + 1, SUB):
                            col[s] = col[s] - factor * scalars[t][s]
                    rest = rest - factor * rows[t]
                strips[g] = rest
                yield
            strip = strip * (recips * lax.rsqrt(recips))
            out.append(jnp.where(lane < first + SUB, strip, 0.0))
            finished.append(jnp.where((lane < first + SUB) | (lane >= SUB * end), strip, 0.0))
        if end < groups:
            rows = jnp.concatenate(finished, axis=0)
            update = mm_tn(rows[:, SUB * end :], rows)
            cleared = (lane >= SUB * opening) & (lane < SUB * end)
            for g in range(end, groups):
                start = SUB * (g - end)
                strips[g] = jnp.where(cleared, 0.0, strips[g]) - update[start : start + SUB, :]
            yield
    return jnp.concatenate(out, axis=0)


def interleave(steps):
    results = [None] * len(steps)
    live = list(range(len(steps)))
    while live:
        for i in list(live):
            try:
                next(steps[i])
            except StopIteration as stop:
                results[i] = stop.value
                live.remove(i)
    return results


def rotate(gram_ref, work):
    lead_ref, trail_ref, first_ref, alone_ref, inv_ref = work

    def close_step():
        lead, trail, lead_inv = lead_ref[...], trail_ref[...], inv_ref[...]
        first = mm(lead_inv, lead)
        corner = mm_nt(mm_nt(trail, lead), lead_inv)
        rest = mm_nt(trail, trail) - mm_nt(corner, corner)
        return first, rest, trail - mm(corner, first)

    def both(iteration, carry):
        first, rest, remainder = close_step()
        lead = mm(first, gram_ref[...])
        lead_inv, trail_inv = interleave(
            [factor_steps(mm_nt(lead, lead), *PAIRED), factor_steps(rest, *PAIRED)]
        )
        lead_ref[...] = lead
        inv_ref[...] = lead_inv
        trail_ref[...] = mm(trail_inv, mm(remainder, gram_ref[...]))
        return carry

    def alone(end, carry):
        inv_ref[...] = interleave([factor_steps(alone_ref[...], *ALONE)])[0]

        @pl.when(end == 0)
        def _():
            lax.fori_loop(0, EIG_ITERS - 1, both, 0)
            first_ref[...], alone_ref[...], trail_ref[...] = close_step()

        return carry

    lead_ref[...] = gram_ref[:BLOCK]
    trail_ref[...] = gram_ref[BLOCK:]
    lead = lead_ref[...]
    alone_ref[...] = mm_nt(lead, lead)
    lax.fori_loop(0, 2, alone, 0)
    return first_ref[...], mm(inv_ref[...], trail_ref[...])


def work_refs():
    tall, square = pltpu.VMEM((BLOCK, 2 * BLOCK), jnp.float32), pltpu.VMEM((BLOCK, BLOCK), jnp.float32)
    return [tall, tall, tall, square, square]


def diagonal_mask(size):
    shape = (size, size)
    return lax.broadcasted_iota(jnp.int32, shape, 0) - lax.broadcasted_iota(jnp.int32, shape, 1)


def diagonal_row(square):
    size = square.shape[0]
    kept = jnp.where(diagonal_mask(size) == 0, square, 0.0)
    return jnp.broadcast_to(jnp.sum(kept, axis=0, keepdims=True), (SUB, size))


def pack(first, second):
    return jnp.where(diagonal_mask(BLOCK) <= 0, first, second)


def unpack(packed, row):
    below = diagonal_mask(BLOCK)
    turned = packed.T
    first = jnp.where(below <= 0, packed, turned)
    second = jnp.where(below > 0, packed, jnp.where(below < 0, turned, jnp.broadcast_to(row, packed.shape)))
    return first, second


def fill_gram(gram_ref, first, cross, second):
    gram_ref[:BLOCK, :BLOCK] = first
    gram_ref[:BLOCK, BLOCK:] = cross
    gram_ref[BLOCK:, :BLOCK] = cross.T
    gram_ref[BLOCK:, BLOCK:] = second


def first_round_kernel(parts_ref, out_ref, gram_ref, *work):
    first, second = unpack(parts_ref[:BLOCK], parts_ref[2 * BLOCK : 2 * BLOCK + 1])
    fill_gram(gram_ref, first, parts_ref[BLOCK : 2 * BLOCK], second)
    gram = gram_ref[...]
    first, second = rotate(gram_ref, work)
    out_ref[:BLOCK] = first
    out_ref[HALF_ROWS : HALF_ROWS + BLOCK] = second
    first = mm_nt(mm(first, gram), first)
    second = mm_nt(mm(second, gram), second)
    packed = pack(first, second)
    for i, (start, lanes) in enumerate(PACK_PLACES):
        out_ref[start : start + PACK, lanes : lanes + BLOCK] = packed[i * PACK : (i + 1) * PACK]
    out_ref[2 * HALF_ROWS :, :BLOCK] = diagonal_row(second)
    out_ref[2 * HALF_ROWS :, BLOCK:] = jnp.zeros((SUB, BLOCK), jnp.float32)


def slot_of(pairing, sweep, block, blocks):
    slot = 0
    for s in range(blocks):
        slot = slot + jnp.where(pairing[sweep, s] == block, s, 0)
    return slot


def part_copies(part, target, sem):
    copies = []
    start = 0
    for piece in part:
        rows = piece.shape[0]
        copies.append(pltpu.make_async_copy(piece, target.at[start : start + rows], sem))
        start += rows
    return copies


def grouped(refs, layout):
    refs = list(refs)
    parts = []
    for pieces in layout:
        parts.append(refs[:pieces])
        refs = refs[pieces:]
    return parts, refs


def second_round_kernel(blocks, layout, total_rows, pairing, ids, *refs):
    parts, (cross_ref, out_ref, turned, gram_ref, sems, *work) = grouped(refs, layout)
    owner = ids[2]
    order = 2 * BLOCK
    slots = [slot_of(pairing, 0, pairing[1, 2 * owner + side], blocks) for side in range(2)]
    for side in range(2):
        wanted = owner ^ (slots[side] // 2)
        for d, part in enumerate(parts):

            @pl.when(wanted == d)
            def _():
                for copy in part_copies(part, turned.at[side], sems.at[side]):
                    copy.start()

    for side in range(2):
        arrive(turned.at[side], sems.at[side])
    halves, owns = [], []
    for side in range(2):
        which = slots[side] % 2
        start = pl.multiple_of(which * HALF_ROWS, SUB)
        halves.append(turned[side, pl.ds(start, BLOCK), :])
        packed = jnp.concatenate(
            [turned[side, at : at + PACK, lanes : lanes + BLOCK] for at, lanes in PACK_PLACES], axis=0
        )
        pair = unpack(packed, turned[side, 2 * HALF_ROWS : 2 * HALF_ROWS + 1, :BLOCK])
        owns.append(jnp.where(which == 0, pair[0], pair[1]))
    cross = mm_nt(mm(halves[0], cross_ref[...]), halves[1])
    fill_gram(gram_ref, owns[0], cross, owns[1])
    gram = gram_ref[...]
    rotation = jnp.concatenate(rotate(gram_ref, work), axis=0)
    squares = mm_nt(mm(rotation, gram), rotation)
    kept = jnp.where(diagonal_mask(order) == 0, squares, 0.0)
    scale = jnp.sqrt(jnp.sum(kept, axis=1, keepdims=True) / total_rows + epsilon)
    out_ref[:order] = rotation / scale
    out_ref[order:] = jnp.sqrt(diagonal_row(squares) / total_rows + epsilon)


def fetch_block(parts, block, target, sem, place, slots):
    wanted = (block // slots) ^ place
    start = pl.multiple_of((block % slots) * BLOCK, BLOCK)
    for d, part in enumerate(parts):

        @pl.when(wanted == d)
        def _():
            pltpu.make_async_copy(part.at[:, pl.ds(start, BLOCK)], target, sem).start()


def arrive(target, sem):
    pltpu.make_async_copy(target, target, sem).wait()


def own_gram_kernel(slots, pairing, ids, *refs):
    *parts, own_ref, other_ref, held, sems = refs
    place, low = ids[0], ids[1]
    tasks = ((other_ref, 1 - low), (own_ref, low))
    for i, (_, s) in enumerate(tasks):
        for side in range(2):
            block = pairing[0, 2 * (place * (slots // 2) + s) + side]
            fetch_block(parts, block, held.at[2 * i + side], sems.at[2 * i + side], place, slots)
    for i, (out_ref, _) in enumerate(tasks):
        for side in range(2):
            arrive(held.at[2 * i + side], sems.at[2 * i + side])
        lead, trail = held[2 * i], held[2 * i + 1]
        second = mm_tn(trail, trail)
        out_ref[:BLOCK] = pack(mm_tn(lead, lead), second)
        out_ref[BLOCK : 2 * BLOCK] = mm_tn(lead, trail)
        out_ref[2 * BLOCK :] = diagonal_row(second)


def cross_gram_kernel(slots, blocks, pairing, ids, *refs):
    *parts, own_ref, other_ref, held, sems = refs
    place, low = ids[0], ids[1]
    tasks = ((other_ref, 1 - low), (own_ref, low))
    for i, (_, s) in enumerate(tasks):
        pair = place * (slots // 2) + s
        for side in range(2):
            source = slot_of(pairing, 0, pairing[1, 2 * pair + side], blocks) // 2
            at = 2 * i + side
            for j in range(2):
                fetch_block(
                    parts,
                    pairing[0, 2 * source + j],
                    held.at[at, :, j * BLOCK : (j + 1) * BLOCK],
                    sems.at[2 * at + j],
                    place,
                    slots,
                )
    for i, (out_ref, _) in enumerate(tasks):
        for at in (2 * i, 2 * i + 1):
            for j in range(2):
                arrive(held.at[at, :, j * BLOCK : (j + 1) * BLOCK], sems.at[2 * at + j])
        out_ref[...] = mm_tn(held[2 * i], held[2 * i + 1])


def first_turn_kernel(slots, places, layout, pairing, ids, *refs):
    parts, rest = refs[:places], refs[places:]
    turned_parts, (out_ref, held, turned, sems) = grouped(rest, layout)
    place, owner = ids[0], ids[2]
    blocks = slots * places
    copies = []
    for d, part in enumerate(turned_parts):
        copies += part_copies(part, turned.at[owner ^ d], sems.at[places + d])
    for d, part in enumerate(parts):
        for j in range(slots):
            copies.append(
                pltpu.make_async_copy(
                    part.at[:, j * BLOCK : (j + 1) * BLOCK], held.at[(place ^ d) * slots + j], sems.at[d]
                )
            )
    for copy in copies:
        copy.start()
    for d in range(len(turned_parts)):
        arrive(turned.at[0], sems.at[places + d])
    for d in range(places):
        arrive(held.at[:slots], sems.at[d])
    for j in range(slots):
        pair = slot_of(pairing, 1, place * slots + j, blocks) // 2
        for side in range(2):
            slot = slot_of(pairing, 0, pairing[1, 2 * pair + side], blocks)
            source = slot // 2
            half = turned[source, pl.ds(pl.multiple_of((slot % 2) * HALF_ROWS, SUB), BLOCK), :]
            joined = jnp.concatenate([held[pairing[0, 2 * source]], held[pairing[0, 2 * source + 1]]], axis=1)
            out_ref[j, :, side * BLOCK : (side + 1) * BLOCK] = mm_nt_three(joined, half)


def last_turn_kernel(slots, blocks, layout, pairing, ids, columns_ref, *refs):
    turned_parts, (left_ref, spec_ref, turned, sems) = grouped(refs, layout)
    place, owner = ids[0], ids[2]
    for d, part in enumerate(turned_parts):
        for copy in part_copies(part, turned.at[owner ^ d], sems.at[d]):
            copy.start()
    for d in range(len(turned_parts)):
        arrive(turned.at[0], sems.at[d])
    for j in range(slots):
        slot = slot_of(pairing, 1, place * slots + j, blocks)
        pair = slot // 2
        start = pl.multiple_of((slot % 2) * BLOCK, BLOCK)
        left_ref[:, j * BLOCK : (j + 1) * BLOCK] = mm_nt_three(
            columns_ref[j], turned[pair, pl.ds(start, BLOCK), :]
        )
        spec_ref[:, j * BLOCK : (j + 1) * BLOCK] = turned[pair, 2 * BLOCK : 2 * BLOCK + 1, pl.ds(start, BLOCK)]


def exchange(x, axis, bit):
    size = lax.axis_size(axis)
    return lax.ppermute(x, axis, [(i, i ^ bit) for i in range(size)])


def gather_pairwise(x):
    result = {0: x}
    bit = lax.axis_size("pair") // 2
    while bit:
        for d, part in list(result.items()):
            result[d ^ bit] = exchange(part, "pair", bit)
        bit //= 2
    return [result[d] for d in range(len(result))]


def gather_owners(x, cut, beside=None):
    far = lax.axis_size("pair") // 2
    across = exchange(x, "row", 1)
    over = exchange(x, "pair", far)
    if beside is not None:
        across, over, beside = lax.optimization_barrier((across, over, beside))
    lower = exchange(across[:cut], "pair", far)
    upper = exchange(over[cut:], "row", 1)
    result = {0: [x], 1: [across], 2 * far: [over], 2 * far + 1: [lower, upper]}
    bit = far // 2
    while bit:
        for d, part in list(result.items()):
            result[d ^ (2 * bit)] = [exchange(piece, "pair", bit) for piece in part]
        bit //= 2
    return [result[d] for d in range(len(result))], beside


def sum_rows(first, second):
    total = first[0] + exchange(first[1], "row", 1)
    total, second = lax.optimization_barrier((total, second))
    behind = (second[0], second[1], 1)
    bit = 2
    while bit < lax.axis_size("row"):
        trailing = behind[0] + exchange(behind[1], "row", behind[2])
        total = total + exchange(total, "row", bit)
        total, trailing = lax.optimization_barrier((total, trailing))
        behind = (trailing, trailing, bit)
        bit *= 2
    return total, behind[0] + exchange(behind[1], "row", behind[2])


vmem = pl.BlockSpec(memory_space=pltpu.VMEM)
smem = pl.BlockSpec(memory_space=pltpu.SMEM)
hbm = pl.BlockSpec(memory_space=pl.ANY)


def call(kernel, in_specs, out_shapes, scratch=(), name=None, flops=0):
    return pl.pallas_call(
        kernel,
        out_shape=[jax.ShapeDtypeStruct(s, jnp.float32) for s in out_shapes],
        in_specs=in_specs,
        out_specs=[vmem] * len(out_shapes),
        scratch_shapes=list(scratch),
        compiler_params=pltpu.CompilerParams(vmem_limit_bytes=VMEM_LIMIT),
        cost_estimate=pl.CostEstimate(flops=flops, bytes_accessed=1 << 20, transcendentals=0),
        name=name,
    )


def flat(parts):
    return [piece for part in parts for piece in part], tuple(len(part) for part in parts)


def shards(snapshots, pairing):
    rows_dev, cols_dev = snapshots.shape
    slots = cols_dev // BLOCK
    places = lax.axis_size("pair")
    blocks = places * slots
    total_rows = rows_dev * lax.axis_size("row")
    order = 2 * BLOCK
    place = lax.axis_index("pair")
    low = lax.axis_index("row") % 2
    ids = jnp.stack([place, low, place * 2 + low]).astype(jnp.int32)

    f32 = jnp.float32
    dma = pltpu.SemaphoreType.DMA
    square = (order, order)
    packed = (order + SUB, BLOCK)
    parts = gather_pairwise(snapshots)
    own_grams = call(
        functools.partial(own_gram_kernel, slots),
        [smem, smem] + [hbm] * places,
        [packed, packed],
        [pltpu.VMEM((4, rows_dev, BLOCK), f32), dma((4,))],
        "own_gram",
    )(pairing, ids, *parts)
    cross_grams = call(
        functools.partial(cross_gram_kernel, slots, blocks),
        [smem, smem] + [hbm] * places,
        [square, square],
        [pltpu.VMEM((4, rows_dev, order), f32), dma((8,))],
        "cross_gram",
        1 << 31,
    )(pairing, ids, *parts)
    own_gram, cross_gram = sum_rows(own_grams, cross_grams)

    chain = 1 << 34
    (turned,) = call(
        first_round_kernel, [vmem], [(STEP_ROWS, order)], [pltpu.VMEM(square, f32)] + work_refs(), "first_round", chain
    )(own_gram)
    turned, cross_gram = lax.optimization_barrier((turned, cross_gram))
    gathered, _ = gather_owners(turned, HALF_ROWS)
    turned_parts, layout = flat(gathered)
    (second,) = call(
        functools.partial(second_round_kernel, blocks, layout, total_rows),
        [smem, smem] + [hbm] * len(turned_parts) + [vmem],
        [(order + SUB, order)],
        [pltpu.VMEM((2, STEP_ROWS, order), f32), pltpu.VMEM(square, f32), dma((2,))] + work_refs(),
        "second_round",
        chain,
    )(pairing, ids, *turned_parts, cross_gram)
    parts, second = lax.optimization_barrier((parts, second))
    (columns,) = call(
        functools.partial(first_turn_kernel, slots, places, layout),
        [smem, smem] + [hbm] * (places + len(turned_parts)),
        [(slots, rows_dev, order)],
        [
            pltpu.VMEM((blocks, rows_dev, BLOCK), f32),
            pltpu.VMEM((len(gathered), STEP_ROWS, order), f32),
            dma((places + len(gathered),)),
        ],
        "first_turn",
        1 << 32,
    )(pairing, ids, *parts, *turned_parts)
    gathered, columns = gather_owners(second, BLOCK, columns)
    second_parts, layout = flat(gathered)
    left, spectrum = call(
        functools.partial(last_turn_kernel, slots, blocks, layout),
        [smem, smem, vmem] + [hbm] * len(second_parts),
        [(rows_dev, cols_dev), (1, cols_dev)],
        [
            pltpu.VMEM((len(gathered), order + SUB, order), f32),
            dma((len(gathered),)),
        ],
        "last_turn",
    )(pairing, ids, columns, *second_parts)
    return left, spectrum.reshape(cols_dev)


def solution(mesh):
    return jax.shard_map(
        shards,
        mesh=mesh,
        in_specs=(P("row", "pair"), P()),
        out_specs=(P("row", "pair"), P("pair")),
        check_vma=False,
    )
```

```python
import functools

import jax
import jax.numpy as jnp
from jax import lax
from jax.experimental import pallas as pl
from jax.experimental.pallas import tpu as pltpu
from jax.sharding import PartitionSpec as P

BLOCK = 128
ROUNDS = 2
EIG_ITERS = 3
SUB = 8

precise = lax.Precision.HIGHEST
epsilon = 1e-06
VMEM_LIMIT = 24 * 1024 * 1024
PACK = BLOCK // 4
HALF_ROWS = BLOCK + PACK
STEP_ROWS = 2 * HALF_ROWS + SUB
PACK_PLACES = ((BLOCK, 0), (BLOCK, BLOCK), (HALF_ROWS + BLOCK, 0), (HALF_ROWS + BLOCK, BLOCK))


def mm(a, b):
    return lax.dot_general(
        a, b, (((1,), (0,)), ((), ())), precision=precise, preferred_element_type=jnp.float32
    )


def mm_nt(a, b):
    return lax.dot_general(
        a, b, (((1,), (1,)), ((), ())), precision=precise, preferred_element_type=jnp.float32
    )


def mm_tn(a, b):
    return lax.dot_general(
        a, b, (((0,), (0,)), ((), ())), precision=precise, preferred_element_type=jnp.float32
    )


def halves_of(x):
    high = x.astype(jnp.bfloat16)
    return high, (x - high.astype(jnp.float32)).astype(jnp.bfloat16)


def mm_nt_three(a, b):
    def one(x, y):
        return lax.dot_general(x, y, (((1,), (1,)), ((), ())), preferred_element_type=jnp.float32)

    (a_high, a_low), (b_high, b_low) = halves_of(a), halves_of(b)
    return one(a_high, b_high) + (one(a_high, b_low) + one(a_low, b_high))


def sub_row(v, t):
    return jnp.broadcast_to(v[t : t + 1, :], v.shape)


def lane_col(v, l):
    return jnp.broadcast_to(v[:, l : l + 1], v.shape)


def inverse_factor(matrix):
    groups, strips_panel = BLOCK // SUB, BLOCK // SUB // 2
    shape = (SUB, BLOCK)
    sub = lax.broadcasted_iota(jnp.int32, shape, 0)
    lane = lax.broadcasted_iota(jnp.int32, shape, 1)
    strips = [matrix[SUB * g : SUB * (g + 1), :] for g in range(groups)]
    out = []
    for opening in range(0, groups, strips_panel):
        end = opening + strips_panel
        next_cols = next_below = None
        finished = []
        for k in range(opening, end):
            first = SUB * k
            inside = (lane >= first) & (lane < first + SUB)
            strip = strips[k]
            cols = next_cols
            if cols is None:
                cols = [lane_col(strip, first + s) for s in range(SUB)]
            below = {}
            for g in range(k + 1, end):
                if g == k + 1 and next_below is not None:
                    below[g] = next_below
                else:
                    below[g] = [lane_col(strips[g], first + s) for s in range(SUB)]
            next_cols = next_below = None
            if k + 1 < end:
                next_cols = [lane_col(strips[k + 1], first + SUB + s) for s in range(SUB)]
            if k + 2 < end:
                next_below = [lane_col(strips[k + 2], first + SUB + s) for s in range(SUB)]
            strip = jnp.where(inside, jnp.where(lane == sub + first, 1.0, 0.0), strip)
            recips = jnp.zeros(shape, jnp.float32)
            recip, scalars, rows = [], [], []
            for t in range(SUB):
                r = 1.0 / sub_row(cols[t], t)
                recips = jnp.where(sub == t, r, recips)
                masked = jnp.where(sub > t, cols[t], 0.0)
                factor = masked * r
                row = sub_row(strip, t)
                scalar = {}
                for s in range(t + 1, SUB):
                    scalar[s] = sub_row(cols[s], t)
                    cols[s] = cols[s] - ((masked * scalar[s]) * r if s == t + 1 else factor * scalar[s])
                if t < SUB - 1:
                    strip = strip - factor * row
                recip.append(r)
                scalars.append(scalar)
                rows.append(row)
                if next_cols is not None:
                    col = below[k + 1]
                    factor = col[t] * r
                    for s in range(t + 1, SUB):
                        col[s] = col[s] - factor * scalar[s]
                    across = [sub_row(col[t], s) for s in range(SUB)]
                    for s in range(SUB):
                        next_cols[s] = next_cols[s] - factor * across[s]
                    if next_below is not None:
                        col = below[k + 2]
                        factor = col[t] * r
                        for s in range(t + 1, SUB):
                            col[s] = col[s] - factor * scalar[s]
                        for s in range(SUB):
                            next_below[s] = next_below[s] - factor * across[s]
            for g in range(k + 1, end):
                col = below[g]
                done = (g == k + 1 and next_cols is not None) or (g == k + 2 and next_below is not None)
                rest = jnp.where(inside, 0.0, strips[g])
                for t in range(SUB):
                    factor = col[t] * recip[t]
                    if not done:
                        for s in range(t + 1, SUB):
                            col[s] = col[s] - factor * scalars[t][s]
                    rest = rest - factor * rows[t]
                strips[g] = rest
            strip = strip * (recips * lax.rsqrt(recips))
            out.append(jnp.where(lane < first + SUB, strip, 0.0))
            finished.append(jnp.where((lane < first + SUB) | (lane >= SUB * end), strip, 0.0))
        if end < groups:
            rows = jnp.concatenate(finished, axis=0)
            update = mm_tn(rows[:, SUB * end :], rows)
            cleared = (lane >= SUB * opening) & (lane < SUB * end)
            for g in range(end, groups):
                start = SUB * (g - end)
                strips[g] = jnp.where(cleared, 0.0, strips[g]) - update[start : start + SUB, :]
    return jnp.concatenate(out, axis=0)


def paired_factors(first, second):
    groups, half = BLOCK // SUB, BLOCK // 2
    panel = groups // 2
    shape = (SUB, BLOCK)
    sub = lax.broadcasted_iota(jnp.int32, shape, 0)
    lane = lax.broadcasted_iota(jnp.int32, shape, 1)
    low = lane < half
    base = jnp.where(low, 0, half)
    lane = lane - base
    left = lax.broadcasted_iota(jnp.int32, (BLOCK, BLOCK), 1) < half

    def regroup(x, y):
        return [jnp.where(left, x, pltpu.roll(y, half, 1)), jnp.where(left, pltpu.roll(x, half, 1), y)]

    def column(v, l):
        return jnp.take_along_axis(v, base + l, axis=1)

    packed = regroup(first, second)
    strips = [[side[SUB * g : SUB * (g + 1)] for side in packed] for g in range(groups)]
    out = []
    for part in range(2):
        opening, end = panel * part, panel * (part + 1)
        next_cols = None
        finished = []
        for k in range(opening, end):
            at = SUB * (k - opening)
            inside = (lane >= at) & (lane < at + SUB)
            strip = list(strips[k])
            cols = next_cols
            if cols is None:
                cols = [column(strip[part], at + s) for s in range(SUB)]
            below = {g: [column(strips[g][part], at + s) for s in range(SUB)] for g in range(k + 1, end)}
            next_cols = None
            if k + 1 < end:
                next_cols = [column(strips[k + 1][part], at + SUB + s) for s in range(SUB)]
            strip[part] = jnp.where(inside, jnp.where(lane == sub + at, 1.0, 0.0), strip[part])
            recips = jnp.zeros(shape, jnp.float32)
            recip, scalars, rows = [], [], []
            for t in range(SUB):
                r = 1.0 / sub_row(cols[t], t)
                recips = jnp.where(sub == t, r, recips)
                masked = jnp.where(sub > t, cols[t], 0.0)
                factor = masked * r
                row = [sub_row(side, t) for side in strip]
                scalar = {}
                for s in range(t + 1, SUB):
                    scalar[s] = sub_row(cols[s], t)
                    cols[s] = cols[s] - ((masked * scalar[s]) * r if s == t + 1 else factor * scalar[s])
                if t < SUB - 1:
                    strip = [side - factor * line for side, line in zip(strip, row)]
                recip.append(r)
                scalars.append(scalar)
                rows.append(row)
                if next_cols is not None:
                    col = below[k + 1]
                    factor = col[t] * r
                    for s in range(t + 1, SUB):
                        col[s] = col[s] - factor * scalar[s]
                    for s in range(SUB):
                        next_cols[s] = next_cols[s] - factor * sub_row(col[t], s)
            for g in range(k + 1, end):
                col = below[g]
                rest = list(strips[g])
                rest[part] = jnp.where(inside, 0.0, rest[part])
                for t in range(SUB):
                    factor = col[t] * recip[t]
                    if g > k + 1:
                        for s in range(t + 1, SUB):
                            col[s] = col[s] - factor * scalars[t][s]
                    rest = [side - factor * line for side, line in zip(rest, rows[t])]
                strips[g] = rest
            scale = recips * lax.rsqrt(recips)
            strip = [side * scale for side in strip]
            kept = jnp.where(lane < at + SUB, strip[part], 0.0)
            out.append([kept, jnp.zeros(shape, jnp.float32)] if part == 0 else [strip[0], kept])
            finished.append([kept, strip[1]])
        if part == 0:
            rows = [jnp.concatenate([strip[i] for strip in finished], axis=0) for i in range(2)]
            for i in range(2):
                update = mm_tn(rows[1], rows[i])
                for g in range(end, groups):
                    start = SUB * (g - end)
                    change = jnp.where(low, update[start : start + SUB], update[half + start : half + start + SUB])
                    strips[g][i] = strips[g][i] - change if i == 1 else -change
    return regroup(*[jnp.concatenate([strip[i] for strip in out], axis=0) for i in range(2)])


def rotate(gram_ref, work):
    lead_ref, trail_ref, first_ref, image_ref, beside_ref, alone_ref, inv_ref = work

    def close_step():
        lead, trail, lead_inv = lead_ref[...], trail_ref[...], inv_ref[...]
        first = mm(lead_inv, lead)
        corner = mm_nt(mm_nt(trail, lead), lead_inv)
        rest = mm_nt(trail, trail) - mm_nt(corner, corner)
        return first, rest, trail - mm(corner, first)

    def both(iteration, carry):
        first, rest, remainder = close_step()
        gram = gram_ref[...]
        lead = mm(first, gram)
        lead_inv, trail_inv = paired_factors(mm_nt(lead, lead), rest)
        lead_ref[...] = lead
        inv_ref[...] = lead_inv
        trail_ref[...] = mm(trail_inv, mm(remainder, gram))
        return carry

    def alone(end, carry):
        gram = gram_ref[...]
        inv_ref[...] = inverse_factor(alone_ref[...])
        image_ref[...] = mm(first_ref[...], gram)
        beside_ref[...] = mm(trail_ref[...], gram)

        @pl.when(end == 0)
        def _():
            lax.fori_loop(0, EIG_ITERS - 1, both, 0)
            first_ref[...], alone_ref[...], trail_ref[...] = close_step()

        return carry

    lead = gram_ref[:BLOCK]
    lead_ref[...] = lead
    trail_ref[...] = gram_ref[BLOCK:]
    first_ref[...] = lead
    alone_ref[...] = mm_nt(lead, lead)
    lax.fori_loop(0, 2, alone, 0)
    inv = inv_ref[...]
    return first_ref[...], image_ref[...], mm(inv, trail_ref[...]), mm(inv, beside_ref[...])


def work_refs():
    tall, square = pltpu.VMEM((BLOCK, 2 * BLOCK), jnp.float32), pltpu.VMEM((BLOCK, BLOCK), jnp.float32)
    return [tall, tall, tall, tall, tall, square, square]


def diagonal_mask(size):
    shape = (size, size)
    return lax.broadcasted_iota(jnp.int32, shape, 0) - lax.broadcasted_iota(jnp.int32, shape, 1)


def diagonal_row(square):
    size = square.shape[0]
    kept = jnp.where(diagonal_mask(size) == 0, square, 0.0)
    return jnp.broadcast_to(jnp.sum(kept, axis=0, keepdims=True), (SUB, size))


def pack(first, second):
    return jnp.where(diagonal_mask(BLOCK) <= 0, first, second)


def unpack(packed, row):
    below = diagonal_mask(BLOCK)
    turned = packed.T
    first = jnp.where(below <= 0, packed, turned)
    second = jnp.where(below > 0, packed, jnp.where(below < 0, turned, jnp.broadcast_to(row, packed.shape)))
    return first, second


def fill_gram(gram_ref, first, cross, second):
    gram_ref[:BLOCK, :BLOCK] = first
    gram_ref[:BLOCK, BLOCK:] = cross
    gram_ref[BLOCK:, :BLOCK] = cross.T
    gram_ref[BLOCK:, BLOCK:] = second


def first_round_kernel(parts_ref, out_ref, gram_ref, *work):
    first, second = unpack(parts_ref[:BLOCK], parts_ref[2 * BLOCK : 2 * BLOCK + 1])
    fill_gram(gram_ref, first, parts_ref[BLOCK : 2 * BLOCK], second)
    first, first_image, second, second_image = rotate(gram_ref, work)
    out_ref[:BLOCK] = first
    out_ref[HALF_ROWS : HALF_ROWS + BLOCK] = second
    first = mm_nt(first_image, first)
    second = mm_nt(second_image, second)
    packed = pack(first, second)
    for i, (start, lanes) in enumerate(PACK_PLACES):
        out_ref[start : start + PACK, lanes : lanes + BLOCK] = packed[i * PACK : (i + 1) * PACK]
    out_ref[2 * HALF_ROWS :, :BLOCK] = diagonal_row(second)
    out_ref[2 * HALF_ROWS :, BLOCK:] = jnp.zeros((SUB, BLOCK), jnp.float32)


def slot_of(pairing, sweep, block, blocks):
    slot = 0
    for s in range(blocks):
        slot = slot + jnp.where(pairing[sweep, s] == block, s, 0)
    return slot


def part_copies(part, target, sem):
    copies = []
    start = 0
    for piece in part:
        rows = piece.shape[0]
        copies.append(pltpu.make_async_copy(piece, target.at[start : start + rows], sem))
        start += rows
    return copies


def grouped(refs, layout):
    refs = list(refs)
    parts = []
    for pieces in layout:
        parts.append(refs[:pieces])
        refs = refs[pieces:]
    return parts, refs


def second_round_kernel(blocks, layout, total_rows, pairing, ids, *refs):
    parts, (kept_ref, other_ref, out_ref, turned, gram_ref, sems, *work) = grouped(refs, layout)
    owner = ids[2]
    order = 2 * BLOCK
    slots = [slot_of(pairing, 0, pairing[1, 2 * owner + side], blocks) for side in range(2)]
    for side in range(2):
        wanted = owner ^ (slots[side] // 2)
        for d, part in enumerate(parts):

            @pl.when(wanted == d)
            def _():
                for copy in part_copies(part, turned.at[side], sems.at[side]):
                    copy.start()

    for side in range(2):
        arrive(turned.at[side], sems.at[side])
    halves, owns = [], []
    for side in range(2):
        which = slots[side] % 2
        start = pl.multiple_of(which * HALF_ROWS, SUB)
        halves.append(turned[side, pl.ds(start, BLOCK), :])
        packed = jnp.concatenate(
            [turned[side, at : at + PACK, lanes : lanes + BLOCK] for at, lanes in PACK_PLACES], axis=0
        )
        pair = unpack(packed, turned[side, 2 * HALF_ROWS : 2 * HALF_ROWS + 1, :BLOCK])
        owns.append(jnp.where(which == 0, pair[0], pair[1]))
    kept, other = kept_ref[...], other_ref[...]
    top = jnp.where(ids[3] == 0, kept, other)
    bottom = jnp.where(ids[3] == 0, other, kept)
    cross = mm_nt(mm(halves[0], jnp.concatenate([top, bottom], axis=0)), halves[1])
    fill_gram(gram_ref, owns[0], cross, owns[1])
    first, first_image, second, second_image = rotate(gram_ref, work)
    for i, (half, image) in enumerate(((first, first_image), (second, second_image))):
        lanes = slice(i * BLOCK, (i + 1) * BLOCK)
        spectrum = jnp.sqrt(jnp.sum(half * image, axis=1, keepdims=True) / total_rows + epsilon)
        out_ref[lanes] = half / spectrum
        out_ref[order:, lanes] = diagonal_row(jnp.broadcast_to(spectrum, (BLOCK, BLOCK)))


def fetch_block(parts, block, target, sem, place, slots):
    wanted = (block // slots) ^ place
    start = pl.multiple_of((block % slots) * BLOCK, BLOCK)
    for d, part in enumerate(parts):

        @pl.when(wanted == d)
        def _():
            pltpu.make_async_copy(part.at[:, pl.ds(start, BLOCK)], target, sem).start()


def arrive(target, sem):
    pltpu.make_async_copy(target, target, sem).wait()


def own_gram_kernel(slots, pairing, ids, *refs):
    *parts, own_ref, other_ref, held, sems = refs
    place, low = ids[0], ids[1]
    tasks = ((other_ref, 1 - low), (own_ref, low))
    for i, (_, s) in enumerate(tasks):
        for side in range(2):
            block = pairing[0, 2 * (place * (slots // 2) + s) + side]
            fetch_block(parts, block, held.at[2 * i + side], sems.at[2 * i + side], place, slots)
    for i, (out_ref, _) in enumerate(tasks):
        for side in range(2):
            arrive(held.at[2 * i + side], sems.at[2 * i + side])
        lead, trail = held[2 * i], held[2 * i + 1]
        second = mm_tn(trail, trail)
        out_ref[:BLOCK] = pack(mm_tn(lead, lead), second)
        out_ref[BLOCK : 2 * BLOCK] = mm_tn(lead, trail)
        out_ref[2 * BLOCK :] = diagonal_row(second)


def cross_gram_kernel(slots, blocks, pairing, ids, *refs):
    *parts, own_ref, other_ref, held, sems = refs
    place, low = ids[0], ids[1]
    tasks = ((other_ref, 1 - low), (own_ref, low))
    for i, (_, s) in enumerate(tasks):
        pair = place * (slots // 2) + s
        for side in range(2):
            source = slot_of(pairing, 0, pairing[1, 2 * pair + side], blocks) // 2
            at = 2 * i + side
            for j in range(2):
                fetch_block(
                    parts,
                    pairing[0, 2 * source + j],
                    held.at[at, :, j * BLOCK : (j + 1) * BLOCK],
                    sems.at[2 * at + j],
                    place,
                    slots,
                )
    for i, (out_ref, _) in enumerate(tasks):
        for at in (2 * i, 2 * i + 1):
            for j in range(2):
                arrive(held.at[at, :, j * BLOCK : (j + 1) * BLOCK], sems.at[2 * at + j])
        for j in range(2):
            start = pl.multiple_of((j ^ ids[3]) * BLOCK, BLOCK)
            out_ref[pl.ds(start, BLOCK)] = mm_tn(held[2 * i, :, j * BLOCK : (j + 1) * BLOCK], held[2 * i + 1])


def first_turn_kernel(slots, places, layout, pairing, ids, *refs):
    parts, rest = refs[:places], refs[places:]
    turned_parts, (out_ref, held, turned, sems) = grouped(rest, layout)
    place, owner = ids[0], ids[2]
    blocks = slots * places
    copies = []
    for d, part in enumerate(turned_parts):
        copies += part_copies(part, turned.at[owner ^ d], sems.at[places + d])
    for d, part in enumerate(parts):
        for j in range(slots):
            copies.append(
                pltpu.make_async_copy(
                    part.at[:, j * BLOCK : (j + 1) * BLOCK], held.at[(place ^ d) * slots + j], sems.at[d]
                )
            )
    for copy in copies:
        copy.start()
    for d in range(len(turned_parts)):
        arrive(turned.at[0], sems.at[places + d])
    for d in range(places):
        arrive(held.at[:slots], sems.at[d])
    for j in range(slots):
        pair = slot_of(pairing, 1, place * slots + j, blocks) // 2
        for side in range(2):
            slot = slot_of(pairing, 0, pairing[1, 2 * pair + side], blocks)
            source = slot // 2
            half = turned[source, pl.ds(pl.multiple_of((slot % 2) * HALF_ROWS, SUB), BLOCK), :]
            joined = jnp.concatenate([held[pairing[0, 2 * source]], held[pairing[0, 2 * source + 1]]], axis=1)
            out_ref[j, :, side * BLOCK : (side + 1) * BLOCK] = mm_nt_three(joined, half)


def last_turn_kernel(slots, blocks, layout, pairing, ids, columns_ref, *refs):
    turned_parts, (left_ref, spec_ref, turned, sems) = grouped(refs, layout)
    place, owner = ids[0], ids[2]
    for d, part in enumerate(turned_parts):
        for copy in part_copies(part, turned.at[owner ^ d], sems.at[d]):
            copy.start()
    for d in range(len(turned_parts)):
        arrive(turned.at[0], sems.at[d])
    for j in range(slots):
        slot = slot_of(pairing, 1, place * slots + j, blocks)
        pair = slot // 2
        start = pl.multiple_of((slot % 2) * BLOCK, BLOCK)
        left_ref[:, j * BLOCK : (j + 1) * BLOCK] = mm_nt_three(
            columns_ref[j], turned[pair, pl.ds(start, BLOCK), :]
        )
        spec_ref[:, j * BLOCK : (j + 1) * BLOCK] = turned[pair, 2 * BLOCK : 2 * BLOCK + 1, pl.ds(start, BLOCK)]


def exchange(x, axis, bit):
    size = lax.axis_size(axis)
    return lax.ppermute(x, axis, [(i, i ^ bit) for i in range(size)])


def gather_pairwise(x):
    result = {0: x}
    bit = lax.axis_size("pair") // 2
    while bit:
        for d, part in list(result.items()):
            result[d ^ bit] = exchange(part, "pair", bit)
        bit //= 2
    return [result[d] for d in range(len(result))]


def gather_owners(x, cut, beside=None, second=None):
    far = lax.axis_size("pair") // 2
    across = exchange(x, "row", 1)
    over = exchange(x, "pair", far)
    result = {0: [x]}
    bit = far // 2
    while bit:
        for d, part in list(result.items()):
            result[d ^ (2 * bit)] = [exchange(piece, "pair", bit) for piece in part]
        bit //= 2
    if beside is None:
        across, over, result = lax.optimization_barrier((across, over, result))
    else:
        across, over, result, beside = lax.optimization_barrier((across, over, result, beside))
    lower = exchange(across[:cut], "pair", far)
    upper = exchange(over[cut:], "row", 1)
    if second is not None:
        beside = (beside, second(beside))
        lower, upper, beside = lax.optimization_barrier((lower, upper, beside))
    later = {1: [across], 2 * far: [over], 2 * far + 1: [lower, upper]}
    bit = far // 2
    while bit:
        for d, part in list(later.items()):
            later[d ^ (2 * bit)] = [exchange(piece, "pair", bit) for piece in part]
        bit //= 2
    result.update(later)
    return [result[d] for d in range(len(result))], beside


def add_across(x, bit):
    return x + exchange(x, "row", bit)


def sum_rows(first, second):
    rows = lax.axis_size("row")
    total = first[0] + exchange(first[1], "row", 1)
    bit = 2
    while bit < rows:
        if 2 * bit >= rows:
            total, second = lax.optimization_barrier((total, second))
        total = add_across(total, bit)
        bit *= 2
    return total, second[0] + exchange(second[1], "row", 1)


vmem = pl.BlockSpec(memory_space=pltpu.VMEM)
smem = pl.BlockSpec(memory_space=pltpu.SMEM)
hbm = pl.BlockSpec(memory_space=pl.ANY)


def call(kernel, in_specs, out_shapes, scratch=(), name=None, flops=0):
    return pl.pallas_call(
        kernel,
        out_shape=[jax.ShapeDtypeStruct(s, jnp.float32) for s in out_shapes],
        in_specs=in_specs,
        out_specs=[vmem] * len(out_shapes),
        scratch_shapes=list(scratch),
        compiler_params=pltpu.CompilerParams(vmem_limit_bytes=VMEM_LIMIT),
        cost_estimate=pl.CostEstimate(flops=flops, bytes_accessed=1 << 20, transcendentals=0),
        name=name,
    )


def flat(parts):
    return [piece for part in parts for piece in part], tuple(len(part) for part in parts)


def shards(snapshots, pairing):
    rows_dev, cols_dev = snapshots.shape
    slots = cols_dev // BLOCK
    places = lax.axis_size("pair")
    blocks = places * slots
    total_rows = rows_dev * lax.axis_size("row")
    order = 2 * BLOCK
    place = lax.axis_index("pair")
    low = lax.axis_index("row") % 2
    keeps = lax.axis_index("row") // 2 % 2
    ids = jnp.stack([place, low, place * 2 + low, keeps]).astype(jnp.int32)

    f32 = jnp.float32
    dma = pltpu.SemaphoreType.DMA
    square = (order, order)
    packed = (order + SUB, BLOCK)
    parts = gather_pairwise(snapshots)
    own_grams = call(
        functools.partial(own_gram_kernel, slots),
        [smem, smem] + [hbm] * places,
        [packed, packed],
        [pltpu.VMEM((4, rows_dev, BLOCK), f32), dma((4,))],
        "own_gram",
    )(pairing, ids, *parts)
    cross_grams = call(
        functools.partial(cross_gram_kernel, slots, blocks),
        [smem, smem] + [hbm] * places,
        [square, square],
        [pltpu.VMEM((4, rows_dev, order), f32), dma((8,))],
        "cross_gram",
        1 << 31,
    )(pairing, ids, *parts)
    own_gram, cross_gram = sum_rows(own_grams, cross_grams)
    own_gram, cross_gram = lax.optimization_barrier((own_gram, cross_gram))
    cross_gram = cross_gram[:BLOCK] + exchange(cross_gram[BLOCK:], "row", 2)

    chain = 1 << 34
    (turned,) = call(
        first_round_kernel, [vmem], [(STEP_ROWS, order)], [pltpu.VMEM(square, f32)] + work_refs(), "first_round", chain
    )(own_gram)
    turned, cross_gram = lax.optimization_barrier((turned, cross_gram))
    bit = 4
    while bit < lax.axis_size("row"):
        cross_gram = add_across(cross_gram, bit)
        bit *= 2
    gathered, (cross_gram, other_cross) = gather_owners(
        turned, HALF_ROWS, cross_gram, lambda x: exchange(x, "row", 2)
    )
    turned_parts, layout = flat(gathered)
    (second,) = call(
        functools.partial(second_round_kernel, blocks, layout, total_rows),
        [smem, smem] + [hbm] * len(turned_parts) + [vmem, vmem],
        [(order + SUB, order)],
        [pltpu.VMEM((2, STEP_ROWS, order), f32), pltpu.VMEM(square, f32), dma((2,))] + work_refs(),
        "second_round",
        chain,
    )(pairing, ids, *turned_parts, cross_gram, other_cross)
    parts, second = lax.optimization_barrier((parts, second))
    (columns,) = call(
        functools.partial(first_turn_kernel, slots, places, layout),
        [smem, smem] + [hbm] * (places + len(turned_parts)),
        [(slots, rows_dev, order)],
        [
            pltpu.VMEM((blocks, rows_dev, BLOCK), f32),
            pltpu.VMEM((len(gathered), STEP_ROWS, order), f32),
            dma((places + len(gathered),)),
        ],
        "first_turn",
        1 << 32,
    )(pairing, ids, *parts, *turned_parts)
    gathered, columns = gather_owners(second, BLOCK, columns)
    second_parts, layout = flat(gathered)
    left, spectrum = call(
        functools.partial(last_turn_kernel, slots, blocks, layout),
        [smem, smem, vmem] + [hbm] * len(second_parts),
        [(rows_dev, cols_dev), (1, cols_dev)],
        [
            pltpu.VMEM((len(gathered), order + SUB, order), f32),
            dma((len(gathered),)),
        ],
        "last_turn",
    )(pairing, ids, columns, *second_parts)
    return left, spectrum.reshape(cols_dev)


def solution(mesh):
    return jax.shard_map(
        shards,
        mesh=mesh,
        in_specs=(P("row", "pair"), P()),
        out_specs=(P("row", "pair"), P("pair")),
        check_vma=False,
    )
```
